32 devices in a mesh: groups: 2 (over y), fsdp: 4 (over z), tp: 2 (over x), sub: 2 (over core).
Axes of the slice: x: 2, y: 2, z: 4, core: 2. Of those that a mesh axis runs over, the one named last changes fastest.
Arguments:
- hidden: bfloat16 [4, 1024, 14336], P(('groups', 'sub'), 'tp', 'fsdp'), parts along dimension 0, may hold values from -6 to 6
- cotangent: bfloat16 [4, 1024, 4096], P(('groups', 'sub'), 'fsdp', 'tp'), parts along dimension 0, may hold values from -6 to 6
- down_projection_weight: bfloat16 [14336, 4096], P('fsdp', 'tp'), may hold values from -0.046875 to 0.046875
- adapter_first_factor: bfloat16 [4, 14336, 64], P('fsdp'), may hold values from -0.046875 to 0.046875
- adapter_second_factor: bfloat16 [4, 64, 4096], P('fsdp', None, 'tp'), may hold values from -0.09375 to 0.09375
- shard_adapter_index: int32 [4, 4, 2], P(('groups', 'sub')), parts along dimension 0, may hold values from 0 to 3, as said below
- member: int32 [4, 1024, 2], P(('groups', 'sub')), parts along dimension 0, may hold values from 0 to 1, as said below
Outputs:
- hidden_grad: bfloat16 [4, 1024, 14336], P(('groups', 'sub'), 'tp', 'fsdp'), parts along dimension 0
- a_grad: float32 [8, 14336, 64], P(('groups', 'fsdp'), None, ('tp', 'sub')), parts along dimension 0
- b_grad: float32 [8, 64, 4096], P(('groups', 'fsdp'), None, ('tp', 'sub')), parts along dimension 0
The draws below stay inside these ranges and needn't reach their ends.
There are 2 independent parts, one for each index of `groups`. The reference program is written for one: setup_inputs(seed, part) draws one part's arguments, and reference() takes and returns one part's arrays. A program takes and returns all parts, laid end to end along the dimension named above; an argument that names none is the same for every part. Nothing has to cross between parts.
Inputs may be any that keep to these rules, and one draw needn't show every extreme that they name: `shard_adapter_index`: the 2 adapters listed for one data shard have different owners (owner = id); some owner appears in every shard's list of the part. `member`: each row has exactly one 1; every slot of every shard's list has rows.
All inputs are finite; a program needn't handle non-finite values.
Results may differ from the reference program's by a relative error of at most 0.015.
Values may be sent and summed in bfloat16 or wider, within the bound.
A program may use at most 192 MiB of HBM per device.

```python
import jax
import jax.numpy as jnp
from jax import lax

MODEL_WIDTH = 4096
FEEDFWD_UNITS = 14336
ADAPTER_RANK = 64
ADPT_DEV = 1
TOK_DEV = 256
ADAPTER_COUNT = 4
SLOTS = 2
ROWS_F = 1024
N_FSDP = 4
N_TP = 2
N_SUB = 2


def draw_shard_adapter_index(key, part):
    key = jax.random.fold_in(key, 11)
    key_common, key_order, key_within = jax.random.split(key, 3)
    shard_count = N_SUB * N_FSDP
    common = jax.random.randint(key_common, (), 0, N_FSDP)
    shard_keys = jax.random.split(key_order, shard_count)

    def one_list(shard_key):
        others = jax.random.permutation(shard_key, N_FSDP - 1)[:SLOTS - 1] + 1
        return jnp.concatenate([jnp.zeros((1,), jnp.int32), others.astype(jnp.int32)])
    offsets = jax.vmap(one_list)(shard_keys)
    owners = (common + offsets) % N_FSDP
    within = jax.random.randint(key_within, (shard_count, SLOTS), 0, ADPT_DEV)
    return (owners * ADPT_DEV + within).reshape(N_SUB, N_FSDP, SLOTS).astype(jnp.int32)


def draw_member(key, part):
    key = jax.random.fold_in(key, 23)
    key_first, key_second = jax.random.split(key, 2)
    first = jax.random.randint(key_first, (N_SUB, ROWS_F), 0, SLOTS)
    second = jax.random.randint(key_second, (N_SUB, ROWS_F), 0, SLOTS)
    selected_adapters = jnp.minimum(first, second)
    position = jnp.arange(ROWS_F) % TOK_DEV
    selected_adapters = jnp.where(position[None, :] < SLOTS, position[None, :], selected_adapters)
    return (selected_adapters[:, :, None] == jnp.arange(SLOTS)[None, None, :]).astype(jnp.int32)


def block_levels(stream_key, extent, cuts, smallest, top_value):
    level = 1.0
    for axis_at, parts in cuts:
        heights = jax.random.uniform(jax.random.fold_in(jax.random.fold_in(stream_key, 6), axis_at), (parts,), jnp.float32, smallest / len(cuts), top_value / len(cuts))
        level = level * jnp.repeat(jnp.exp(heights), extent[axis_at] // parts).reshape((-1,) + (1,) * (len(extent) - 1 - axis_at))
    return level


def scatter_about(own_key, shape, scale, bound, cuts=(), dtype=jnp.bfloat16):
    entries = scale * jax.random.normal(own_key, shape, jnp.float32)
    if cuts:
        entries = entries * block_levels(own_key, shape, cuts, -0.22, 0.18)
    return jnp.clip(entries, -bound, bound).astype(dtype)


def setup_inputs(seed: int = 0, part: int = 0) -> dict:
    splits = jax.random.split(jax.random.key(seed), 8)
    part_keys = jax.random.split(jax.random.fold_in(splits[7], part), 8)
    hidden = scatter_about(part_keys[0], (N_SUB, ROWS_F, FEEDFWD_UNITS), 1.0, 6.0, ((0, 2), (1, 2), (2, 4)))
    cotangent = scatter_about(part_keys[1], (N_SUB, ROWS_F, MODEL_WIDTH), 1.0, 6.0, ((0, 2), (1, 4), (2, 2)))
    down_projection_weight = scatter_about(splits[2], (FEEDFWD_UNITS, MODEL_WIDTH), FEEDFWD_UNITS ** -0.5, 0.046875, ((0, 4), (1, 2)))
    adapter_first_factor = scatter_about(splits[3], (ADAPTER_COUNT, FEEDFWD_UNITS, ADAPTER_RANK), FEEDFWD_UNITS ** -0.5, 0.046875, ((0, 4),))
    adapter_second_factor = scatter_about(splits[4], (ADAPTER_COUNT, ADAPTER_RANK, MODEL_WIDTH), MODEL_WIDTH ** -0.5, 0.09375, ((0, 4), (2, 2)))
    shard_adapter_index = draw_shard_adapter_index(jax.random.fold_in(jax.random.fold_in(splits[7], part), 71), part)
    member = draw_member(jax.random.fold_in(jax.random.fold_in(splits[7], part), 71), part)
    return dict(hidden=hidden, cotangent=cotangent, down_projection_weight=down_projection_weight, adapter_first_factor=adapter_first_factor, adapter_second_factor=adapter_second_factor, shard_adapter_index=shard_adapter_index, member=member)


adapter_scale = 2.0


def reference(hidden, cotangent, down_projection_weight, adapter_first_factor, adapter_second_factor, shard_adapter_index, member):
    shard_count = N_SUB * N_FSDP
    block_width = MODEL_WIDTH // N_TP
    hidden_rows = hidden.reshape(shard_count, TOK_DEV, FEEDFWD_UNITS)
    upstream_rows = cotangent.reshape(shard_count, TOK_DEV, MODEL_WIDTH)
    slot_table = shard_adapter_index.reshape(shard_count, SLOTS).astype(jnp.int32)
    slot_marks = member.reshape(shard_count, TOK_DEV, SLOTS)

    def one_shard(totals, inputs):
        grad_a, grad_b = totals
        hidden_block, incoming_gradient, selected_adapters, row_marks = inputs
        marks_float = row_marks.astype(jnp.float32)
        marks_half = row_marks.astype(jnp.bfloat16)
        selected_first = jnp.take(adapter_first_factor, selected_adapters, axis=0).astype(jnp.float32)
        selected_second = jnp.take(adapter_second_factor, selected_adapters, axis=0)
        adjoint_sum = jnp.zeros((TOK_DEV, ADAPTER_RANK), jnp.float32)
        frozen_total = jnp.zeros((TOK_DEV, FEEDFWD_UNITS), jnp.float32)
        for block_pos in range(N_TP):
            first_col = block_pos * block_width
            part_up = incoming_gradient[:, first_col:first_col + block_width]
            part_b = selected_second[:, :, first_col:first_col + block_width]
            slot_adjoint = jnp.einsum("td,krd->tkr", part_up.astype(jnp.float32), part_b.astype(jnp.float32))
            part_adjoint = jnp.sum(slot_adjoint * marks_float[:, :, None], axis=1).astype(jnp.bfloat16)
            part_base = jnp.dot(part_up, down_projection_weight[:, first_col:first_col + block_width].T, preferred_element_type=jnp.float32).astype(jnp.bfloat16)
            part_adjoint, part_base = lax.optimization_barrier((part_adjoint, part_base))
            adjoint_sum = adjoint_sum + part_adjoint.astype(jnp.float32)
            frozen_total = frozen_total + part_base.astype(jnp.float32)
        adjoint_half = adjoint_sum.astype(jnp.bfloat16)
        adjoint_full_width = (marks_half[:, :, None] * adjoint_half[:, None, :]).astype(jnp.float32)
        low_rank_contribution = jnp.einsum("tkr,kfr->tf", adjoint_full_width, selected_first)
        hidden_gradient = (frozen_total + adapter_scale * low_rank_contribution).astype(jnp.bfloat16)
        hidden_single_precision = hidden_block.astype(jnp.float32)
        latent_slots = jnp.einsum("tf,kfr->tkr", hidden_single_precision, selected_first)
        latent_half = jnp.sum(latent_slots * marks_float[:, :, None], axis=1).astype(jnp.bfloat16)
        latent_full_width = (marks_half[:, :, None] * latent_half[:, None, :]).astype(jnp.float32)
        slot_second_gradients = adapter_scale * jnp.einsum("mgu,mz->guz", latent_full_width, incoming_gradient.astype(jnp.float32))
        slot_first_gradients = adapter_scale * jnp.einsum("dc,dhu->hcu", hidden_single_precision, adjoint_full_width)
        grad_a = grad_a.at[selected_adapters].add(slot_first_gradients)
        grad_b = grad_b.at[selected_adapters].add(slot_second_gradients)
        return (grad_a, grad_b), hidden_gradient

    start_totals = (jnp.zeros((ADAPTER_COUNT, FEEDFWD_UNITS, ADAPTER_RANK), jnp.float32), jnp.zeros((ADAPTER_COUNT, ADAPTER_RANK, MODEL_WIDTH), jnp.float32))
    (grad_a, grad_b), grads_h = lax.scan(one_shard, start_totals, (hidden_rows, upstream_rows, slot_table, slot_marks))
    return grads_h.reshape(N_SUB, ROWS_F, FEEDFWD_UNITS), grad_a, grad_b
```

```python
import jax
import jax.numpy as jnp
from jax import lax
from jax.sharding import PartitionSpec as P

adapter_scale = 2.0


def take_block(x, pos, count, dim):
    size = x.shape[dim] // count
    return lax.dynamic_slice_in_dim(x, pos * size, size, dim)


def swap(x, axis):
    return lax.ppermute(x, axis, [(0, 1), (1, 0)])


def scatter_sum(x, axis, dim):
    n = lax.axis_size(axis)
    if n != 2:
        return lax.psum_scatter(
            x.astype(jnp.bfloat16), axis, scatter_dimension=dim, tiled=True
        ).astype(jnp.float32)
    pos = lax.axis_index(axis)
    away = take_block(x, 1 - pos, 2, dim).astype(jnp.bfloat16)
    return take_block(x, pos, 2, dim) + swap(away, axis).astype(jnp.float32)


def gather(x, axis, dim):
    n = lax.axis_size(axis)
    if n != 2:
        return lax.all_gather(x, axis, axis=dim, tiled=True)
    other = swap(x, axis)
    first = lax.axis_index(axis) == 0
    return jnp.concatenate(
        [jnp.where(first, x, other), jnp.where(first, other, x)], axis=dim
    )


def base_sum(incoming_gradient, weight):
    rows_up = lax.all_gather(incoming_gradient, "fsdp", axis=0, tiled=True)
    tp = lax.axis_size("tp")
    tp_pos = lax.axis_index("tp")
    dims = (((1,), (1,)), ((), ()))
    if tp != 2:
        base = lax.dot_general(rows_up, weight, dims, preferred_element_type=jnp.float32)
        return lax.psum_scatter(
            base.astype(jnp.bfloat16), "tp", scatter_dimension=0, tiled=True
        ).astype(jnp.float32)
    away = take_block(rows_up, 1 - tp_pos, 2, 0)
    mine = take_block(rows_up, tp_pos, 2, 0)
    arrived = []
    for part in range(4):
        rows = away.shape[0] // 4
        block = lax.dot_general(
            away[part * rows:(part + 1) * rows], weight, dims,
            preferred_element_type=jnp.float32,
        ).astype(jnp.bfloat16)
        arrived.append(swap(block, "tp"))
    own = lax.dot_general(mine, weight, dims, preferred_element_type=jnp.float32)
    own = own.astype(jnp.bfloat16).astype(jnp.float32)
    return own + jnp.concatenate(arrived, axis=0).astype(jnp.float32)


def shards(
    hidden,
    cotangent,
    down_projection_weight,
    adapter_first_factor,
    adapter_second_factor,
    shard_adapter_index,
    member,
):
    fsdp = lax.axis_size("fsdp")
    tp = lax.axis_size("tp")
    sub = lax.axis_size("sub")
    f = lax.axis_index("fsdp")
    t = lax.axis_index("tp")
    s = lax.axis_index("sub")
    rows = cotangent.shape[1]
    rows_all = rows * fsdp
    block_rows = hidden.shape[1]
    units = hidden.shape[2]
    own, _, rank = adapter_first_factor.shape
    adapters = own * fsdp
    up = cotangent[0]
    hid = hidden[0]

    ids = shard_adapter_index[0]
    hits = (
        member[0].reshape(fsdp, rows, -1, 1)
        * (ids[:, None, :, None] == jnp.arange(adapters)).astype(jnp.int32)
    ).sum(axis=2).reshape(rows_all, adapters)
    hits_shard = take_block(hits, f, fsdp, 0)
    hits_block = take_block(hits, t, tp, 0)

    def widen(low, marks):
        return (
            jnp.broadcast_to(low[:, None, :], (low.shape[0], adapters, rank))
            * marks[:, :, None].astype(low.dtype)
        ).reshape(low.shape[0], adapters * rank)

    def narrow(wide, marks):
        return jnp.sum(
            wide.reshape(-1, adapters, rank) * marks[:, :, None].astype(wide.dtype), axis=1
        )

    second = take_block(adapter_second_factor, s, sub, 2)
    second = gather(lax.all_gather(second, "fsdp", axis=0, tiled=True), "sub", 2)
    second = second.reshape(adapters * rank, -1)
    first = take_block(jnp.swapaxes(adapter_first_factor, 1, 2), s, sub, 1)
    first = lax.all_to_all(first, "fsdp", split_axis=2, concat_axis=0, tiled=True)
    first = gather(first, "sub", 1).reshape(adapters * rank, units)

    base = base_sum(up, down_projection_weight)

    qpart = narrow(
        lax.dot_general(up, second, (((1,), (1,)), ((), ())), preferred_element_type=jnp.float32),
        hits_shard,
    ).astype(jnp.bfloat16)
    if tp == 2:
        q = (qpart.astype(jnp.float32) + swap(qpart, "tp").astype(jnp.float32)).astype(jnp.bfloat16)
    else:
        q = lax.psum(qpart, "tp")
    q_all = lax.all_gather(q, "fsdp", axis=0, tiled=True)
    q_wide = widen(take_block(q_all, t, tp, 0), hits_block)

    u = narrow(
        lax.dot_general(hid, first, (((1,), (1,)), ((), ())), preferred_element_type=jnp.float32),
        hits_block,
    ).astype(jnp.bfloat16)
    u = gather(lax.psum(u, "fsdp"), "tp", 0)
    u_wide = widen(take_block(u, f, fsdp, 0), hits_shard)

    part_a = adapter_scale * lax.dot_general(
        q_wide, hid, (((0,), (0,)), ((), ())), preferred_element_type=jnp.float32
    )
    part_a = part_a.reshape(adapters, tp, sub, rank // (tp * sub), units)
    part_a = scatter_sum(scatter_sum(part_a, "sub", 2), "tp", 1)
    part_a = part_a.reshape(adapters, rank // (tp * sub), units).astype(jnp.bfloat16)
    grad_a = lax.all_to_all(part_a, "fsdp", split_axis=0, concat_axis=2, tiled=True)
    grad_a = jnp.swapaxes(grad_a.astype(jnp.float32), 1, 2)

    part_b = adapter_scale * lax.dot_general(
        u_wide, up, (((0,), (0,)), ((), ())), preferred_element_type=jnp.float32
    )
    part_b = scatter_sum(part_b, "sub", 1).astype(jnp.bfloat16)
    grad_b = lax.psum_scatter(part_b, "fsdp", scatter_dimension=0, tiled=True)
    grad_b = grad_b.reshape(own, rank, -1).astype(jnp.float32)

    low = lax.dot_general(
        q_wide, first, (((1,), (0,)), ((), ())), preferred_element_type=jnp.float32
    )
    hidden_gradient = (base + adapter_scale * low).astype(jnp.bfloat16)[None]
    return (hidden_gradient, grad_a, grad_b)


def solution(mesh):
    placed = (
        P(("groups", "sub"), "tp", "fsdp"),
        P(("groups", "sub"), "fsdp", "tp"),
        P("fsdp", "tp"),
        P("fsdp", None, None),
        P("fsdp", None, "tp"),
        P(("groups", "sub"), None, None),
        P(("groups", "sub"), None, None),
    )
    return jax.shard_map(
        shards,
        mesh=mesh,
        in_specs=placed,
        out_specs=(
            P(("groups", "sub"), "tp", "fsdp"),
            P(("groups", "fsdp"), None, ("tp", "sub")),
            P(("groups", "fsdp"), None, ("tp", "sub")),
        ),
        check_vma=False,
    )
```

```python
import jax
import jax.numpy as jnp
from jax import lax
from jax.experimental import pallas as pl
from jax.experimental.pallas import tpu as pltpu
from jax.sharding import PartitionSpec as P

adapter_scale = 2.0


def take_block(x, pos, count, dim):
    size = x.shape[dim] // count
    return lax.dynamic_slice_in_dim(x, pos * size, size, dim)


def swap(x, axis):
    return lax.ppermute(x, axis, [(0, 1), (1, 0)])


def scatter_sum(x, axis, dim):
    n = lax.axis_size(axis)
    if n != 2:
        return lax.psum_scatter(
            x.astype(jnp.bfloat16), axis, scatter_dimension=dim, tiled=True
        ).astype(jnp.float32)
    pos = lax.axis_index(axis)
    away = take_block(x, 1 - pos, 2, dim).astype(jnp.bfloat16)
    return take_block(x, pos, 2, dim) + swap(away, axis).astype(jnp.float32)


def gather(x, axis, dim):
    n = lax.axis_size(axis)
    if n != 2:
        return lax.all_gather(x, axis, axis=dim, tiled=True)
    other = swap(x, axis)
    first = lax.axis_index(axis) == 0
    return jnp.concatenate(
        [jnp.where(first, x, other), jnp.where(first, other, x)], axis=dim
    )


MESH = pl.DeviceIdType.MESH
TILE = 512


def base_kernel(
    cot_ref, w_ref, own_ref, arr_ref,
    held, weight, stage, own_sem, w_sem, recv_sem, right_sem, left_sem, out_sem, in_sem,
):
    f = lax.axis_index("fsdp")
    t = lax.axis_index("tp")
    rows = cot_ref.shape[0]
    tiles = w_ref.shape[0] // TILE

    load = pltpu.make_async_copy(cot_ref, held.at[f], own_sem)
    load.start()
    barrier = pltpu.get_barrier_semaphore()
    for peer in ({"fsdp": (f + 1) % 4}, {"fsdp": (f + 3) % 4}, {"tp": 1 - t}):
        pl.semaphore_signal(barrier, inc=1, device_id=peer, device_id_type=MESH)
    pl.semaphore_wait(barrier, 3)
    load.wait()

    def rightward(p):
        return pltpu.make_async_remote_copy(
            held.at[p], held.at[p], right_sem.at[p], recv_sem.at[p],
            device_id={"fsdp": (f + 1) % 4}, device_id_type=MESH,
        )

    def leftward(p):
        return pltpu.make_async_remote_copy(
            held.at[p], held.at[p], left_sem.at[p], recv_sem.at[p],
            device_id={"fsdp": (f + 3) % 4}, device_id_type=MESH,
        )

    def across(slot):
        return pltpu.make_async_remote_copy(
            stage.at[slot], arr_ref.at[slot], out_sem.at[slot], in_sem.at[slot],
            device_id={"tp": 1 - t}, device_id_type=MESH,
        )

    def w_copy(tile):
        span = pl.ds(pl.multiple_of(tile * TILE, TILE), TILE)
        return pltpu.make_async_copy(w_ref.at[span], weight.at[span], w_sem.at[tile])

    upper = f // 2
    near = f + upper * (3 - 2 * f)

    def step(i, carry):
        middle = ((i + 1) % 3) * (1 - i // 3) + 3 * (i // 3)
        p = (1 - near) * i + near * middle
        p = p + upper * (3 - 2 * p)

        @pl.when(i > 0)
        def _():
            rightward(p).wait_recv()

        @pl.when((p <= f) & (f < 3))
        def _():
            rightward(p).start()

        @pl.when((p >= f) & (f > 0))
        def _():
            leftward(p).start()

        @pl.when(i == 0)
        def _():
            lax.fori_loop(0, tiles, lambda k, c: (w_copy(k).start(), c)[1], 0)

        slot = p % 2
        mine = (p // 2) == t

        def tile_step(k, c):
            @pl.when(i == 0)
            def _():
                w_copy(k).wait()

            span = pl.ds(pl.multiple_of(k * TILE, TILE), TILE)
            block = lax.dot_general(
                held[p], weight[span, :], (((1,), (1,)), ((), ())),
                preferred_element_type=jnp.float32,
            ).astype(jnp.bfloat16)

            @pl.when(mine)
            def _():
                own_ref[slot, :, span] = block

            @pl.when(jnp.logical_not(mine))
            def _():
                stage[slot, :, span] = block
            return c

        lax.fori_loop(0, tiles, tile_step, 0)

        @pl.when(jnp.logical_not(mine))
        def _():
            across(slot).start()
        return carry

    lax.fori_loop(0, 4, step, 0)

    def drain(p, c):
        @pl.when((p <= f) & (f < 3))
        def _():
            rightward(p).wait_send()

        @pl.when((p >= f) & (f > 0))
        def _():
            leftward(p).wait_send()
        return c

    lax.fori_loop(0, 4, drain, 0)
    for slot in range(2):
        across(slot).wait()


def base_parts(up, weight):
    rows, width = up.shape
    units = weight.shape[0]
    fsdp, tp = lax.axis_size("fsdp"), lax.axis_size("tp")
    if fsdp == 4 and tp == 2 and units % TILE == 0:
        half = jax.ShapeDtypeStruct((2, rows, units), jnp.bfloat16)
        own, arrived = pl.pallas_call(
            base_kernel,
            out_shape=(half, half),
            in_specs=[pl.BlockSpec(memory_space=pl.ANY)] * 2,
            out_specs=[pl.BlockSpec(memory_space=pltpu.VMEM)] * 2,
            scratch_shapes=[
                pltpu.VMEM((4, rows, width), jnp.bfloat16),
                pltpu.VMEM((units, width), jnp.bfloat16),
                pltpu.VMEM((2, rows, units), jnp.bfloat16),
                pltpu.SemaphoreType.DMA,
                pltpu.SemaphoreType.DMA((units // TILE,)),
                pltpu.SemaphoreType.DMA((4,)),
                pltpu.SemaphoreType.DMA((4,)),
                pltpu.SemaphoreType.DMA((4,)),
                pltpu.SemaphoreType.DMA((2,)),
                pltpu.SemaphoreType.DMA((2,)),
            ],
            compiler_params=pltpu.CompilerParams(
                collective_id=0, has_side_effects=True, vmem_limit_bytes=48 * 2**20
            ),
            cost_estimate=pl.CostEstimate(
                flops=8 * rows * width * units,
                bytes_accessed=2 * units * width + 8 * rows * units,
                transcendentals=0,
            ),
        )(up, weight)
        return own.reshape(2 * rows, units), arrived.reshape(2 * rows, units)
    rows_up = lax.all_gather(up, "fsdp", axis=0, tiled=True)
    base = lax.dot_general(
        rows_up, weight, (((1,), (1,)), ((), ())), preferred_element_type=jnp.float32
    )
    return (lax.psum_scatter(base.astype(jnp.bfloat16), "tp", scatter_dimension=0, tiled=True),)


def shards(
    hidden,
    cotangent,
    down_projection_weight,
    adapter_first_factor,
    adapter_second_factor,
    shard_adapter_index,
    member,
):
    fsdp = lax.axis_size("fsdp")
    tp = lax.axis_size("tp")
    sub = lax.axis_size("sub")
    f = lax.axis_index("fsdp")
    t = lax.axis_index("tp")
    s = lax.axis_index("sub")
    rows = cotangent.shape[1]
    rows_all = rows * fsdp
    block_rows = hidden.shape[1]
    units = hidden.shape[2]
    own, _, rank = adapter_first_factor.shape
    adapters = own * fsdp
    up = cotangent[0]
    hid = hidden[0]

    ids = shard_adapter_index[0]
    hits = (
        member[0].reshape(fsdp, rows, -1, 1)
        * (ids[:, None, :, None] == jnp.arange(adapters)).astype(jnp.int32)
    ).sum(axis=2).reshape(rows_all, adapters)
    hits_shard = take_block(hits, f, fsdp, 0)
    hits_block = take_block(hits, t, tp, 0)

    def widen(low, marks):
        return (
            jnp.broadcast_to(low[:, None, :], (low.shape[0], adapters, rank))
            * marks[:, :, None].astype(low.dtype)
        ).reshape(low.shape[0], adapters * rank)

    def narrow(wide, marks):
        return jnp.sum(
            wide.reshape(-1, adapters, rank) * marks[:, :, None].astype(wide.dtype), axis=1
        )

    second = take_block(adapter_second_factor, s, sub, 2)
    second = gather(lax.all_gather(second, "fsdp", axis=0, tiled=True), "sub", 2)
    second = second.reshape(adapters * rank, -1)
    first = take_block(jnp.swapaxes(adapter_first_factor, 1, 2), s, sub, 1)
    first = jnp.concatenate([first[:, :, k * units:(k + 1) * units] for k in range(fsdp)], axis=0)
    first = lax.all_to_all(
        first.reshape(fsdp, own, rank // sub, units), "fsdp", split_axis=0, concat_axis=0
    ).reshape(adapters, rank // sub, units)
    first = gather(first, "sub", 1).reshape(adapters * rank, units)

    base = sum(x.astype(jnp.float32) for x in base_parts(up, down_projection_weight))

    qpart = narrow(
        lax.dot_general(up, second, (((1,), (1,)), ((), ())), preferred_element_type=jnp.float32),
        hits_shard,
    ).astype(jnp.bfloat16)
    if tp == 2:
        q = (qpart.astype(jnp.float32) + swap(qpart, "tp").astype(jnp.float32)).astype(jnp.bfloat16)
    else:
        q = lax.psum(qpart, "tp")
    q_all = lax.all_gather(q, "fsdp", axis=0, tiled=True)
    q_wide = widen(take_block(q_all, t, tp, 0), hits_block)

    u = narrow(
        lax.dot_general(hid, first, (((1,), (1,)), ((), ())), preferred_element_type=jnp.float32),
        hits_block,
    ).astype(jnp.bfloat16)
    u = gather(lax.psum(u, "fsdp"), "tp", 0)
    u_wide = widen(take_block(u, f, fsdp, 0), hits_shard)

    part_a = adapter_scale * lax.dot_general(
        q_wide, hid, (((0,), (0,)), ((), ())), preferred_element_type=jnp.float32
    )
    part_a = part_a.reshape(adapters, tp, sub, rank // (tp * sub), units)
    part_a = scatter_sum(scatter_sum(part_a, "sub", 2), "tp", 1)
    part_a = part_a.reshape(adapters, rank // (tp * sub), units).astype(jnp.bfloat16)
    grad_a = lax.all_to_all(part_a, "fsdp", split_axis=0, concat_axis=2, tiled=True)
    grad_a = jnp.swapaxes(grad_a.astype(jnp.float32), 1, 2)

    part_b = adapter_scale * lax.dot_general(
        u_wide, up, (((0,), (0,)), ((), ())), preferred_element_type=jnp.float32
    )
    part_b = scatter_sum(part_b, "sub", 1).astype(jnp.bfloat16)
    grad_b = lax.psum_scatter(part_b, "fsdp", scatter_dimension=0, tiled=True)
    grad_b = grad_b.reshape(own, rank, -1).astype(jnp.float32)

    low = lax.dot_general(
        q_wide, first, (((1,), (0,)), ((), ())), preferred_element_type=jnp.float32
    )
    hidden_gradient = (base + adapter_scale * low).astype(jnp.bfloat16)[None]
    return (hidden_gradient, grad_a, grad_b)


def solution(mesh):
    placed = (
        P(("groups", "sub"), "tp", "fsdp"),
        P(("groups", "sub"), "fsdp", "tp"),
        P("fsdp", "tp"),
        P("fsdp", None, None),
        P("fsdp", None, "tp"),
        P(("groups", "sub"), None, None),
        P(("groups", "sub"), None, None),
    )
    return jax.shard_map(
        shards,
        mesh=mesh,
        in_specs=placed,
        out_specs=(
            P(("groups", "sub"), "tp", "fsdp"),
            P(("groups", "fsdp"), None, ("tp", "sub")),
            P(("groups", "fsdp"), None, ("tp", "sub")),
        ),
        check_vma=False,
    )
```

```python
import jax
import jax.numpy as jnp
from jax import lax
from jax.experimental import pallas as pl
from jax.experimental.pallas import tpu as pltpu
from jax.sharding import PartitionSpec as P

adapter_scale = 2.0


def take_block(x, pos, count, dim):
    size = x.shape[dim] // count
    return lax.dynamic_slice_in_dim(x, pos * size, size, dim)


def swap(x, axis):
    return lax.ppermute(x, axis, [(0, 1), (1, 0)])


def scatter_sum(x, axis, dim):
    n = lax.axis_size(axis)
    if n != 2:
        return lax.psum_scatter(
            x.astype(jnp.bfloat16), axis, scatter_dimension=dim, tiled=True
        ).astype(jnp.float32)
    pos = lax.axis_index(axis)
    away = take_block(x, 1 - pos, 2, dim).astype(jnp.bfloat16)
    return take_block(x, pos, 2, dim) + swap(away, axis).astype(jnp.float32)


def gather(x, axis, dim):
    n = lax.axis_size(axis)
    if n != 2:
        return lax.all_gather(x, axis, axis=dim, tiled=True)
    other = swap(x, axis)
    first = lax.axis_index(axis) == 0
    return jnp.concatenate(
        [jnp.where(first, x, other), jnp.where(first, other, x)], axis=dim
    )


MESH = pl.DeviceIdType.MESH
TILE = 512


def base_kernel(
    cot_ref, w_ref, own_ref, arr_ref,
    held, weight, stage, own_sem, w_sem, recv_sem, right_sem, left_sem, out_sem, in_sem,
):
    f = lax.axis_index("fsdp")
    t = lax.axis_index("tp")
    rows = cot_ref.shape[0]
    tiles = w_ref.shape[0] // TILE

    load = pltpu.make_async_copy(cot_ref, held.at[f], own_sem)
    load.start()
    barrier = pltpu.get_barrier_semaphore()
    for peer in ({"fsdp": (f + 1) % 4}, {"fsdp": (f + 3) % 4}, {"tp": 1 - t}):
        pl.semaphore_signal(barrier, inc=1, device_id=peer, device_id_type=MESH)
    pl.semaphore_wait(barrier, 3)
    load.wait()

    def rightward(p):
        return pltpu.make_async_remote_copy(
            held.at[p], held.at[p], right_sem.at[p], recv_sem.at[p],
            device_id={"fsdp": (f + 1) % 4}, device_id_type=MESH,
        )

    def leftward(p):
        return pltpu.make_async_remote_copy(
            held.at[p], held.at[p], left_sem.at[p], recv_sem.at[p],
            device_id={"fsdp": (f + 3) % 4}, device_id_type=MESH,
        )

    def across(slot, tile):
        span = pl.ds(pl.multiple_of(tile * TILE, TILE), TILE)
        return pltpu.make_async_remote_copy(
            stage.at[slot, :, span], arr_ref.at[slot, :, span],
            out_sem.at[slot, tile], in_sem.at[slot, tile],
            device_id={"tp": 1 - t}, device_id_type=MESH,
        )

    def w_copy(tile):
        span = pl.ds(pl.multiple_of(tile * TILE, TILE), TILE)
        return pltpu.make_async_copy(w_ref.at[span], weight.at[span], w_sem.at[tile])

    upper = f // 2
    near = f + upper * (3 - 2 * f)

    def step(i, carry):
        middle = ((i + 1) % 3) * (1 - i // 3) + 3 * (i // 3)
        p = (1 - near) * i + near * middle
        p = p + upper * (3 - 2 * p)

        @pl.when(i > 0)
        def _():
            rightward(p).wait_recv()

        @pl.when((p <= f) & (f < 3))
        def _():
            rightward(p).start()

        @pl.when((p >= f) & (f > 0))
        def _():
            leftward(p).start()

        @pl.when(i == 0)
        def _():
            lax.fori_loop(0, tiles, lambda k, c: (w_copy(k).start(), c)[1], 0)

        slot = p % 2
        mine = (p // 2) == t

        def tile_step(k, c):
            @pl.when(i == 0)
            def _():
                w_copy(k).wait()

            span = pl.ds(pl.multiple_of(k * TILE, TILE), TILE)
            block = lax.dot_general(
                held[p], weight[span, :], (((1,), (1,)), ((), ())),
                preferred_element_type=jnp.float32,
            ).astype(jnp.bfloat16)

            @pl.when(mine)
            def _():
                own_ref[slot, :, span] = block

            @pl.when(jnp.logical_not(mine))
            def _():
                stage[slot, :, span] = block
                across(slot, k).start()
            return c

        lax.fori_loop(0, tiles, tile_step, 0)
        return carry

    lax.fori_loop(0, 4, step, 0)

    def drain(p, c):
        @pl.when((p <= f) & (f < 3))
        def _():
            rightward(p).wait_send()

        @pl.when((p >= f) & (f > 0))
        def _():
            leftward(p).wait_send()
        return c

    lax.fori_loop(0, 4, drain, 0)
    for slot in range(2):
        lax.fori_loop(0, tiles, lambda k, c, slot=slot: (across(slot, k).wait(), c)[1], 0)


def base_parts(up, weight):
    rows, width = up.shape
    units = weight.shape[0]
    fsdp, tp = lax.axis_size("fsdp"), lax.axis_size("tp")
    if fsdp == 4 and tp == 2 and units % TILE == 0:
        half = jax.ShapeDtypeStruct((2, rows, units), jnp.bfloat16)
        own, arrived = pl.pallas_call(
            base_kernel,
            out_shape=(half, half),
            in_specs=[pl.BlockSpec(memory_space=pl.ANY)] * 2,
            out_specs=[pl.BlockSpec(memory_space=pltpu.VMEM)] * 2,
            scratch_shapes=[
                pltpu.VMEM((4, rows, width), jnp.bfloat16),
                pltpu.VMEM((units, width), jnp.bfloat16),
                pltpu.VMEM((2, rows, units), jnp.bfloat16),
                pltpu.SemaphoreType.DMA,
                pltpu.SemaphoreType.DMA((units // TILE,)),
                pltpu.SemaphoreType.DMA((4,)),
                pltpu.SemaphoreType.DMA((4,)),
                pltpu.SemaphoreType.DMA((4,)),
                pltpu.SemaphoreType.DMA((2, units // TILE)),
                pltpu.SemaphoreType.DMA((2, units // TILE)),
            ],
            compiler_params=pltpu.CompilerParams(
                collective_id=0, has_side_effects=True, vmem_limit_bytes=48 * 2**20
            ),
            cost_estimate=pl.CostEstimate(
                flops=64 * rows * width * units,
                bytes_accessed=2 * units * width + 8 * rows * units,
                transcendentals=0,
            ),
        )(up, weight)
        return own.reshape(2 * rows, units), arrived.reshape(2 * rows, units)
    rows_up = lax.all_gather(up, "fsdp", axis=0, tiled=True)
    base = lax.dot_general(
        rows_up, weight, (((1,), (1,)), ((), ())), preferred_element_type=jnp.float32
    )
    return (lax.psum_scatter(base.astype(jnp.bfloat16), "tp", scatter_dimension=0, tiled=True),)


def shards(
    hidden,
    cotangent,
    down_projection_weight,
    adapter_first_factor,
    adapter_second_factor,
    shard_adapter_index,
    member,
):
    fsdp = lax.axis_size("fsdp")
    tp = lax.axis_size("tp")
    sub = lax.axis_size("sub")
    f = lax.axis_index("fsdp")
    t = lax.axis_index("tp")
    s = lax.axis_index("sub")
    rows = cotangent.shape[1]
    rows_all = rows * fsdp
    block_rows = hidden.shape[1]
    units = hidden.shape[2]
    own, _, rank = adapter_first_factor.shape
    adapters = own * fsdp
    up = cotangent[0]
    hid = hidden[0]

    ids = shard_adapter_index[0]
    hits = (
        member[0].reshape(fsdp, rows, -1, 1)
        * (ids[:, None, :, None] == jnp.arange(adapters)).astype(jnp.int32)
    ).sum(axis=2).reshape(rows_all, adapters)
    hits_shard = take_block(hits, f, fsdp, 0)
    hits_block = take_block(hits, t, tp, 0)

    def widen(low, marks):
        return (
            jnp.broadcast_to(low[:, None, :], (low.shape[0], adapters, rank))
            * marks[:, :, None].astype(low.dtype)
        ).reshape(low.shape[0], adapters * rank)

    def narrow(wide, marks):
        return jnp.sum(
            wide.reshape(-1, adapters, rank) * marks[:, :, None].astype(wide.dtype), axis=1
        )

    first = take_block(jnp.swapaxes(adapter_first_factor, 1, 2), s, sub, 1)
    first = jnp.concatenate([first[:, :, k * units:(k + 1) * units] for k in range(fsdp)], axis=0)
    first = lax.all_to_all(
        first.reshape(fsdp, own, rank // sub, units), "fsdp", split_axis=0, concat_axis=0
    ).reshape(adapters, rank // sub, units)
    first = gather(first, "sub", 1).reshape(adapters * rank, units)
    second = take_block(adapter_second_factor, s, sub, 2)
    second = gather(lax.all_gather(second, "fsdp", axis=0, tiled=True), "sub", 2)
    second = second.reshape(adapters * rank, -1)

    qpart = narrow(
        lax.dot_general(up, second, (((1,), (1,)), ((), ())), preferred_element_type=jnp.float32),
        hits_shard,
    ).astype(jnp.bfloat16)
    if tp == 2:
        q = (qpart.astype(jnp.float32) + swap(qpart, "tp").astype(jnp.float32)).astype(jnp.bfloat16)
    else:
        q = lax.psum(qpart, "tp")
    q_all = lax.all_gather(q, "fsdp", axis=0, tiled=True)
    q_wide = widen(take_block(q_all, t, tp, 0), hits_block)

    u_part = narrow(
        lax.dot_general(hid, first, (((1,), (1,)), ((), ())), preferred_element_type=jnp.float32),
        hits_block,
    ).astype(jnp.bfloat16)

    part_a = adapter_scale * lax.dot_general(
        q_wide, hid, (((0,), (0,)), ((), ())), preferred_element_type=jnp.float32
    )
    part_a = part_a.reshape(adapters, tp, sub, rank // (tp * sub), units)
    part_a = scatter_sum(scatter_sum(part_a, "sub", 2), "tp", 1)
    part_a = part_a.reshape(adapters, rank // (tp * sub), units).astype(jnp.bfloat16)

    up_base, u_part, part_a = lax.optimization_barrier((up, u_part, part_a))
    u = lax.psum(u_part, "fsdp")
    grad_a = lax.all_to_all(part_a, "fsdp", split_axis=0, concat_axis=2, tiled=True)
    bases = base_parts(up_base, down_projection_weight)
    bases, u, grad_a = lax.optimization_barrier((bases, u, grad_a))
    base = sum(x.astype(jnp.float32) for x in bases)
    grad_a = jnp.swapaxes(grad_a.astype(jnp.float32), 1, 2)

    u = gather(u, "tp", 0)
    u_wide = widen(take_block(u, f, fsdp, 0), hits_shard)
    part_b = adapter_scale * lax.dot_general(
        u_wide, up, (((0,), (0,)), ((), ())), preferred_element_type=jnp.float32
    )
    part_b = scatter_sum(part_b, "sub", 1).astype(jnp.bfloat16)
    grad_b = lax.psum_scatter(part_b, "fsdp", scatter_dimension=0, tiled=True)
    grad_b = grad_b.reshape(own, rank, -1).astype(jnp.float32)

    low = lax.dot_general(
        q_wide, first, (((1,), (0,)), ((), ())), preferred_element_type=jnp.float32
    )
    hidden_gradient = (base + adapter_scale * low).astype(jnp.bfloat16)[None]
    return (hidden_gradient, grad_a, grad_b)


def solution(mesh):
    placed = (
        P(("groups", "sub"), "tp", "fsdp"),
        P(("groups", "sub"), "fsdp", "tp"),
        P("fsdp", "tp"),
        P("fsdp", None, None),
        P("fsdp", None, "tp"),
        P(("groups", "sub"), None, None),
        P(("groups", "sub"), None, None),
    )
    return jax.shard_map(
        shards,
        mesh=mesh,
        in_specs=placed,
        out_specs=(
            P(("groups", "sub"), "tp", "fsdp"),
            P(("groups", "fsdp"), None, ("tp", "sub")),
            P(("groups", "fsdp"), None, ("tp", "sub")),
        ),
        check_vma=False,
    )
```

```python
import jax
import jax.numpy as jnp
from jax import lax
from jax.experimental import pallas as pl
from jax.experimental.pallas import tpu as pltpu
from jax.sharding import PartitionSpec as P

adapter_scale = 2.0


def take_block(x, pos, count, dim):
    size = x.shape[dim] // count
    return lax.dynamic_slice_in_dim(x, pos * size, size, dim)


def swap(x, axis):
    return lax.ppermute(x, axis, [(0, 1), (1, 0)])


def scatter_sum(x, axis, dim):
    n = lax.axis_size(axis)
    if n != 2:
        return lax.psum_scatter(
            x.astype(jnp.bfloat16), axis, scatter_dimension=dim, tiled=True
        ).astype(jnp.float32)
    pos = lax.axis_index(axis)
    away = take_block(x, 1 - pos, 2, dim).astype(jnp.bfloat16)
    return take_block(x, pos, 2, dim) + swap(away, axis).astype(jnp.float32)


def gather(x, axis, dim):
    n = lax.axis_size(axis)
    if n != 2:
        return lax.all_gather(x, axis, axis=dim, tiled=True)
    other = swap(x, axis)
    first = lax.axis_index(axis) == 0
    return jnp.concatenate(
        [jnp.where(first, x, other), jnp.where(first, other, x)], axis=dim
    )


MESH = pl.DeviceIdType.MESH
TILE = 512


def base_kernel(
    cot_ref, w_ref, own_ref, arr_ref,
    held, weight, stage, own_sem, w_sem, recv_sem, right_sem, left_sem, out_sem, in_sem,
):
    f = lax.axis_index("fsdp")
    t = lax.axis_index("tp")
    rows = cot_ref.shape[0]
    tiles = w_ref.shape[0] // TILE

    load = pltpu.make_async_copy(cot_ref, held.at[f], own_sem)
    load.start()
    barrier = pltpu.get_barrier_semaphore()
    for peer in ({"fsdp": (f + 1) % 4}, {"fsdp": (f + 3) % 4}, {"tp": 1 - t}):
        pl.semaphore_signal(barrier, inc=1, device_id=peer, device_id_type=MESH)
    pl.semaphore_wait(barrier, 3)
    load.wait()

    def rightward(p):
        return pltpu.make_async_remote_copy(
            held.at[p], held.at[p], right_sem.at[p], recv_sem.at[p],
            device_id={"fsdp": (f + 1) % 4}, device_id_type=MESH,
        )

    def leftward(p):
        return pltpu.make_async_remote_copy(
            held.at[p], held.at[p], left_sem.at[p], recv_sem.at[p],
            device_id={"fsdp": (f + 3) % 4}, device_id_type=MESH,
        )

    def across(slot, tile):
        span = pl.ds(pl.multiple_of(tile * TILE, TILE), TILE)
        return pltpu.make_async_remote_copy(
            stage.at[slot, :, span], arr_ref.at[slot, :, span],
            out_sem.at[slot, tile], in_sem.at[slot, tile],
            device_id={"tp": 1 - t}, device_id_type=MESH,
        )

    def w_copy(tile):
        span = pl.ds(pl.multiple_of(tile * TILE, TILE), TILE)
        return pltpu.make_async_copy(w_ref.at[span], weight.at[span], w_sem.at[tile])

    upper = f // 2
    near = f + upper * (3 - 2 * f)

    def step(i, carry):
        middle = ((i + 1) % 3) * (1 - i // 3) + 3 * (i // 3)
        p = (1 - near) * i + near * middle
        p = p + upper * (3 - 2 * p)

        @pl.when(i > 0)
        def _():
            rightward(p).wait_recv()

        @pl.when((p <= f) & (f < 3))
        def _():
            rightward(p).start()

        @pl.when((p >= f) & (f > 0))
        def _():
            leftward(p).start()

        @pl.when(i == 0)
        def _():
            lax.fori_loop(0, tiles, lambda k, c: (w_copy(k).start(), c)[1], 0)

        slot = p % 2
        mine = (p // 2) == t

        def tile_step(k, c):
            @pl.when(i == 0)
            def _():
                w_copy(k).wait()

            span = pl.ds(pl.multiple_of(k * TILE, TILE), TILE)
            block = lax.dot_general(
                held[p], weight[span, :], (((1,), (1,)), ((), ())),
                preferred_element_type=jnp.float32,
            ).astype(jnp.bfloat16)

            @pl.when(mine)
            def _():
                own_ref[slot, :, span] = block

            @pl.when(jnp.logical_not(mine))
            def _():
                stage[slot, :, span] = block
                across(slot, k).start()
            return c

        lax.fori_loop(0, tiles, tile_step, 0)
        return carry

    lax.fori_loop(0, 4, step, 0)

    def drain(p, c):
        @pl.when((p <= f) & (f < 3))
        def _():
            rightward(p).wait_send()

        @pl.when((p >= f) & (f > 0))
        def _():
            leftward(p).wait_send()
        return c

    lax.fori_loop(0, 4, drain, 0)
    for slot in range(2):
        lax.fori_loop(0, tiles, lambda k, c, slot=slot: (across(slot, k).wait(), c)[1], 0)


def base_parts(up, weight):
    rows, width = up.shape
    units = weight.shape[0]
    fsdp, tp = lax.axis_size("fsdp"), lax.axis_size("tp")
    if fsdp == 4 and tp == 2 and units % TILE == 0:
        half = jax.ShapeDtypeStruct((2, rows, units), jnp.bfloat16)
        own, arrived = pl.pallas_call(
            base_kernel,
            out_shape=(half, half),
            in_specs=[pl.BlockSpec(memory_space=pl.ANY)] * 2,
            out_specs=[pl.BlockSpec(memory_space=pltpu.VMEM)] * 2,
            scratch_shapes=[
                pltpu.VMEM((4, rows, width), jnp.bfloat16),
                pltpu.VMEM((units, width), jnp.bfloat16),
                pltpu.VMEM((2, rows, units), jnp.bfloat16),
                pltpu.SemaphoreType.DMA,
                pltpu.SemaphoreType.DMA((units // TILE,)),
                pltpu.SemaphoreType.DMA((4,)),
                pltpu.SemaphoreType.DMA((4,)),
                pltpu.SemaphoreType.DMA((4,)),
                pltpu.SemaphoreType.DMA((2, units // TILE)),
                pltpu.SemaphoreType.DMA((2, units // TILE)),
            ],
            compiler_params=pltpu.CompilerParams(
                collective_id=0, has_side_effects=True, vmem_limit_bytes=48 * 2**20
            ),
            cost_estimate=pl.CostEstimate(
                flops=64 * rows * width * units,
                bytes_accessed=2 * units * width + 8 * rows * units,
                transcendentals=0,
            ),
        )(up, weight)
        return own.reshape(2 * rows, units), arrived.reshape(2 * rows, units)
    rows_up = lax.all_gather(up, "fsdp", axis=0, tiled=True)
    base = lax.dot_general(
        rows_up, weight, (((1,), (1,)), ((), ())), preferred_element_type=jnp.float32
    )
    return (lax.psum_scatter(base.astype(jnp.bfloat16), "tp", scatter_dimension=0, tiled=True),)


def factor_kernel(first_ref, second_ref, first_out, second_out, send_sem, recv_sem, own_sem):
    f = lax.axis_index("fsdp")
    barrier = pltpu.get_barrier_semaphore()
    for d in range(1, 4):
        pl.semaphore_signal(
            barrier, inc=1, device_id={"fsdp": (f + d) % 4}, device_id_type=MESH
        )
    pl.semaphore_wait(barrier, 3)
    copies = []
    for d in (1, 2, 3):
        to = (f + d) % 4
        for kind, (source, target) in enumerate(
            ((second_ref, second_out.at[f]), (first_ref.at[to], first_out.at[f]))
        ):
            copies.append(
                pltpu.make_async_remote_copy(
                    source, target, send_sem.at[kind, d - 1], recv_sem.at[kind, d - 1],
                    device_id={"fsdp": to}, device_id_type=MESH,
                )
            )
    copies.append(pltpu.make_async_copy(second_ref, second_out.at[f], own_sem.at[0]))
    copies.append(pltpu.make_async_copy(first_ref.at[f], first_out.at[f], own_sem.at[1]))
    for copy in copies:
        copy.start()
    for copy in copies:
        copy.wait()


def exchange_factors(first, second):
    fsdp = first.shape[0]
    if fsdp == 4:
        vmem = pl.BlockSpec(memory_space=pltpu.VMEM)
        return pl.pallas_call(
            factor_kernel,
            out_shape=(
                jax.ShapeDtypeStruct(first.shape, first.dtype),
                jax.ShapeDtypeStruct((fsdp,) + second.shape, second.dtype),
            ),
            in_specs=[vmem] * 2,
            out_specs=[vmem] * 2,
            scratch_shapes=[
                pltpu.SemaphoreType.DMA((2, 3)),
                pltpu.SemaphoreType.DMA((2, 3)),
                pltpu.SemaphoreType.DMA((2,)),
            ],
            compiler_params=pltpu.CompilerParams(
                collective_id=1, has_side_effects=True, vmem_limit_bytes=24 * 2**20
            ),
        )(first, second)
    first = lax.all_to_all(first, "fsdp", split_axis=0, concat_axis=0)
    return first, lax.all_gather(second, "fsdp", axis=0)


def shards(
    hidden,
    cotangent,
    down_projection_weight,
    adapter_first_factor,
    adapter_second_factor,
    shard_adapter_index,
    member,
):
    fsdp = lax.axis_size("fsdp")
    tp = lax.axis_size("tp")
    sub = lax.axis_size("sub")
    f = lax.axis_index("fsdp")
    t = lax.axis_index("tp")
    s = lax.axis_index("sub")
    rows = cotangent.shape[1]
    rows_all = rows * fsdp
    block_rows = hidden.shape[1]
    units = hidden.shape[2]
    own, _, rank = adapter_first_factor.shape
    adapters = own * fsdp
    up = cotangent[0]
    hid = hidden[0]

    ids = shard_adapter_index[0]
    hits = (
        member[0].reshape(fsdp, rows, -1, 1)
        * (ids[:, None, :, None] == jnp.arange(adapters)).astype(jnp.int32)
    ).sum(axis=2).reshape(rows_all, adapters)
    hits_shard = take_block(hits, f, fsdp, 0)
    hits_block = take_block(hits, t, tp, 0)

    def widen(low, marks):
        return (
            jnp.broadcast_to(low[:, None, :], (low.shape[0], adapters, rank))
            * marks[:, :, None].astype(low.dtype)
        ).reshape(low.shape[0], adapters * rank)

    def narrow(wide, marks):
        return jnp.sum(
            wide.reshape(-1, adapters, rank) * marks[:, :, None].astype(wide.dtype), axis=1
        )

    first = take_block(jnp.swapaxes(adapter_first_factor, 1, 2), s, sub, 1)
    first = jnp.concatenate([first[:, :, k * units:(k + 1) * units] for k in range(fsdp)], axis=0)
    second = take_block(adapter_second_factor, s, sub, 2)
    first, second = exchange_factors(
        first.reshape(fsdp, own * (rank // sub), units), second.reshape(own * rank, -1)
    )
    first = gather(first.reshape(adapters, rank // sub, units), "sub", 1)
    first = first.reshape(adapters * rank, units)
    second = gather(second.reshape(adapters, rank, -1), "sub", 2).reshape(adapters * rank, -1)

    qpart = narrow(
        lax.dot_general(up, second, (((1,), (1,)), ((), ())), preferred_element_type=jnp.float32),
        hits_shard,
    ).astype(jnp.bfloat16)
    if tp == 2:
        q = (qpart.astype(jnp.float32) + swap(qpart, "tp").astype(jnp.float32)).astype(jnp.bfloat16)
    else:
        q = lax.psum(qpart, "tp")
    q_all = lax.all_gather(q, "fsdp", axis=0, tiled=True)
    q_wide = widen(take_block(q_all, t, tp, 0), hits_block)

    u_part = narrow(
        lax.dot_general(hid, first, (((1,), (1,)), ((), ())), preferred_element_type=jnp.float32),
        hits_block,
    ).astype(jnp.bfloat16)

    part_a = adapter_scale * lax.dot_general(
        q_wide, hid, (((0,), (0,)), ((), ())), preferred_element_type=jnp.float32
    )
    part_a = part_a.reshape(adapters, tp, sub, rank // (tp * sub), units)
    part_a = scatter_sum(scatter_sum(part_a, "sub", 2), "tp", 1)
    part_a = part_a.reshape(adapters, rank // (tp * sub), units).astype(jnp.bfloat16)

    up_base, u_part, part_a = lax.optimization_barrier((up, u_part, part_a))
    u = lax.psum(u_part, "fsdp")
    grad_a = lax.all_to_all(part_a, "fsdp", split_axis=0, concat_axis=2, tiled=True)
    bases = base_parts(up_base, down_projection_weight)
    bases, u, grad_a = lax.optimization_barrier((bases, u, grad_a))
    base = sum(x.astype(jnp.float32) for x in bases)
    grad_a = jnp.swapaxes(grad_a.astype(jnp.float32), 1, 2)

    u = gather(u, "tp", 0)
    u_wide = widen(take_block(u, f, fsdp, 0), hits_shard)
    part_b = adapter_scale * lax.dot_general(
        u_wide, up, (((0,), (0,)), ((), ())), preferred_element_type=jnp.float32
    )
    part_b = scatter_sum(part_b, "sub", 1).astype(jnp.bfloat16)
    grad_b = lax.psum_scatter(part_b, "fsdp", scatter_dimension=0, tiled=True)
    grad_b = grad_b.reshape(own, rank, -1).astype(jnp.float32)

    low = lax.dot_general(
        q_wide, first, (((1,), (0,)), ((), ())), preferred_element_type=jnp.float32
    )
    hidden_gradient = (base + adapter_scale * low).astype(jnp.bfloat16)[None]
    return (hidden_gradient, grad_a, grad_b)


def solution(mesh):
    placed = (
        P(("groups", "sub"), "tp", "fsdp"),
        P(("groups", "sub"), "fsdp", "tp"),
        P("fsdp", "tp"),
        P("fsdp", None, None),
        P("fsdp", None, "tp"),
        P(("groups", "sub"), None, None),
        P(("groups", "sub"), None, None),
    )
    return jax.shard_map(
        shards,
        mesh=mesh,
        in_specs=placed,
        out_specs=(
            P(("groups", "sub"), "tp", "fsdp"),
            P(("groups", "fsdp"), None, ("tp", "sub")),
            P(("groups", "fsdp"), None, ("tp", "sub")),
        ),
        check_vma=False,
    )
```
